32 devices in a mesh: grp: 1, dap: 32 (over z, y, x, core), sub: 1.
Axes of the slice: x: 2, y: 2, z: 4, core: 2. Of those that a mesh axis runs over, the one named last changes fastest.
Arguments:
- pair: bfloat16 [128, 128, 128], P(('grp', 'dap'), 'sub'), may hold values from -6 to 6
- pair_mask: int32 [128, 128], P(('grp', 'dap'), 'sub'), may hold values 0 or 1
- ln_gain: float32 [128], replicated, may hold values from 0.1 to 1.9
- ln_bias: float32 [128], replicated, may hold values from -3 to 3
- w_proj: bfloat16 [128, 512], replicated, may hold values from -0.5 to 0.5
- w_gate: bfloat16 [128, 128], replicated, may hold values from -0.5 to 0.5
- tri_gain: float32 [128], replicated, may hold values from 0.1 to 1.9
- tri_bias: float32 [128], replicated, may hold values from -3 to 3
- w_out: bfloat16 [128, 128], replicated, may hold values from -0.5 to 0.5
Outputs:
- update: bfloat16 [128, 128, 128], P(('grp', 'dap'), 'sub')
The draws below stay inside these ranges and needn't reach their ends.
All inputs are finite; a program needn't handle non-finite values. No bound on the sum of `pair_mask` on one device may be relied on, other than what follows from the above.
Results may differ from the reference program's by a relative error of at most 0.018.
Values may be sent and summed in bfloat16 or wider, within the bound.
A program may use at most 64 MiB of HBM per device.

```python
import jax
import jax.numpy as jnp
from jax import lax

C = 128
H = 128
ROWS_DEV = 4
N = 128
N_DAP = 32


def with_ends(values, stream_key, least, top_value):
    shape = values.shape
    index_at = [jax.random.randint(jax.random.fold_in(stream_key, axis), (), 0, shape[axis]) for axis in range(len(shape))]
    values = values.at[tuple(index_at)].set(least)
    longest = shape.index(max(shape))
    index_at[longest] = (index_at[longest] + 1) % shape[longest]
    return values.at[tuple(index_at)].set(top_value)


def block_levels(own_key, shape, pieces, smallest, largest):
    factor_of = 1.0
    for position, blocks in pieces:
        steps = jax.random.uniform(jax.random.fold_in(jax.random.fold_in(own_key, 6), position), (blocks,), jnp.float32, smallest / len(pieces), largest / len(pieces))
        factor_of = factor_of * jnp.repeat(jnp.exp(steps), shape[position] // blocks).reshape((-1,) + (1,) * (len(shape) - 1 - position))
    return factor_of


def bell_draw(key, extent, deviation, most, shards=(), kind=jnp.bfloat16):
    level = block_levels(key, extent, shards, -0.22, 0.18) if shards else 1.0
    result = jax.random.normal(key, extent, jnp.float32) * deviation * level
    return jnp.minimum(jnp.maximum(result, -most), most).astype(kind)


def setup_inputs(seed: int = 0, part: int = 0) -> dict:
    seeds = jax.random.split(jax.random.key(seed), 10)
    part_splits = jax.random.split(jax.random.fold_in(seeds[9], part), 10)
    return {
        "pair": bell_draw(part_splits[0], (N, N, C), 1.0, 6.0, ((0, 32),)),
        "pair_mask": with_ends((jax.random.randint(part_splits[1], (N, N), 0, 8) < 7).astype(jnp.int32), jax.random.fold_in(part_splits[1], 1), 0, 1),
        "ln_gain": jnp.clip(1.0 + 0.18 * jax.random.normal(seeds[2], (C,), jnp.float32), 0.1, 1.9),
        "ln_bias": bell_draw(seeds[3], (C,), 0.5, 3.0, (), jnp.float32),
        "w_proj": bell_draw(seeds[4], (C, 4 * H), C ** -0.5, 0.5),
        "w_gate": bell_draw(seeds[5], (C, C), C ** -0.5, 0.5),
        "tri_gain": jnp.clip(1.0 + 0.18 * jax.random.normal(seeds[6], (H,), jnp.float32), 0.1, 1.9),
        "tri_bias": bell_draw(seeds[7], (H,), 0.5, 3.0, (), jnp.float32),
        "w_out": bell_draw(seeds[8], (H, C), H ** -0.5, 0.5),
    }


def layer_norm(values, gain, bias, axis):
    mean = lax.optimization_barrier(jnp.mean(values, axis=axis, keepdims=True))
    var = lax.optimization_barrier(jnp.mean((values - mean) ** 2, axis=axis, keepdims=True))
    return (values - mean) * lax.rsqrt(var + 1e-05) * gain + bias

def reference(pair, pair_mask, ln_gain, ln_bias, w_proj, w_gate, tri_gain, tri_bias, w_out):
    high = lax.Precision.HIGHEST
    row_blocks = pair.reshape(N_DAP, ROWS_DEV, N, C)
    mask_blocks = pair_mask.reshape(N_DAP, ROWS_DEV, N)
    proj_w = w_proj.astype(jnp.float32)

    def project(args):
        block, mblock = args
        normed = layer_norm(block.astype(jnp.float32), ln_gain, ln_bias, -1).astype(jnp.bfloat16)
        proj = jnp.einsum('rkc,cd->drk', normed.astype(jnp.float32), proj_w, precision=high)
        maskf = mblock.astype(jnp.float32)
        left = (jax.nn.sigmoid(proj[0:H]) * proj[H:2 * H] * maskf).astype(jnp.bfloat16)
        right = (jax.nn.sigmoid(proj[2 * H:3 * H]) * proj[3 * H:4 * H] * maskf).astype(jnp.bfloat16)
        return (left, right)
    left, right = lax.map(project, (row_blocks, mask_blocks))
    left = jnp.transpose(left, (1, 0, 2, 3)).reshape(H, N, N)
    right = jnp.transpose(right, (1, 0, 2, 3)).reshape(H, N, N)
    half = N // 2

    def channel(args):
        lchan, rchan = args
        lchan = lchan.astype(jnp.float32)
        rchan = rchan.astype(jnp.float32)
        first = jnp.dot(lchan[:, :half], rchan[:, :half].T, precision=high, preferred_element_type=jnp.float32)
        second = jnp.dot(lchan[:, half:], rchan[:, half:].T, precision=high, preferred_element_type=jnp.float32)
        first = lax.optimization_barrier(first.astype(jnp.bfloat16)).astype(jnp.float32)
        second = lax.optimization_barrier(second.astype(jnp.bfloat16)).astype(jnp.float32)
        return (first + second).astype(jnp.bfloat16)
    tri = lax.map(channel, (left, right))
    tri_blocks = jnp.transpose(tri.reshape(H, N_DAP, ROWS_DEV, N), (1, 0, 2, 3))
    gate_w = w_gate.astype(jnp.float32)
    out_w = w_out.astype(jnp.float32)

    def finish(args):
        block, tblock = args
        normed = layer_norm(block.astype(jnp.float32), ln_gain, ln_bias, -1).astype(jnp.bfloat16)
        out_gate = jax.nn.sigmoid(jnp.einsum('rjc,cd->rjd', normed.astype(jnp.float32), gate_w, precision=high))
        tri_normed = layer_norm(tblock.astype(jnp.float32), tri_gain[:, None, None], tri_bias[:, None, None], 0).astype(jnp.bfloat16)
        linear = jnp.einsum('crj,cd->rjd', tri_normed.astype(jnp.float32), out_w, precision=high)
        return (out_gate * linear).astype(jnp.bfloat16)
    update = lax.map(finish, (row_blocks, tri_blocks))
    return update.reshape(N, N, C)
```

```python
import functools

import jax
import jax.numpy as jnp
from jax import lax
from jax.experimental import pallas as pl
from jax.experimental.pallas import tpu as pltpu
from jax.sharding import PartitionSpec as P

MESH = pl.DeviceIdType.MESH
GROUP = 4


def layer_norm(values, gain, bias, axis):
    mean = jnp.mean(values, axis=axis, keepdims=True)
    var = jnp.mean((values - mean) ** 2, axis=axis, keepdims=True)
    return (values - mean) * lax.rsqrt(var + 1e-05) * gain + bias


def body(pair, pair_mask, ln_gain, ln_bias, w_proj, w_gate, tri_gain, tri_bias, w_out):
    hidden = w_out.shape[0]
    normed = layer_norm(pair.astype(jnp.float32), ln_gain, ln_bias, -1).astype(jnp.bfloat16)
    proj = jnp.einsum("rkc,cd->drk", normed, w_proj, preferred_element_type=jnp.float32)
    maskf = pair_mask.astype(jnp.float32)
    left = (jax.nn.sigmoid(proj[0:hidden]) * proj[hidden : 2 * hidden] * maskf).astype(jnp.bfloat16)
    right = (
        jax.nn.sigmoid(proj[2 * hidden : 3 * hidden]) * proj[3 * hidden : 4 * hidden] * maskf
    ).astype(jnp.bfloat16)
    left_all, right_all = (
        lax.all_to_all(left, "dap", split_axis=0, concat_axis=1, tiled=True),
        lax.all_to_all(right, "dap", split_axis=0, concat_axis=1, tiled=True),
    )
    out_gate = jax.nn.sigmoid(
        jnp.einsum("rjc,cd->rjd", normed, w_gate, preferred_element_type=jnp.float32)
    )
    partial_value = jnp.einsum(
        "hjk,hik->hij", right_all, left_all, preferred_element_type=jnp.float32
    ).astype(jnp.bfloat16)
    moved = lax.all_to_all(partial_value, "dap", split_axis=1, concat_axis=0, tiled=True)
    tri = lax.psum_scatter(
        moved.astype(jnp.float32).astype(jnp.bfloat16), "sub", scatter_dimension=2, tiled=True
    )
    tri_normed = layer_norm(
        tri.astype(jnp.float32), tri_gain[:, None, None], tri_bias[:, None, None], 0
    ).astype(jnp.bfloat16)
    linear = jnp.einsum("crj,cd->rjd", tri_normed, w_out, preferred_element_type=jnp.float32)
    return (out_gate * linear).astype(jnp.bfloat16)


def sigmoid(x):
    return 0.5 * jnp.tanh(0.5 * x) + 0.5


def interleave(parts):
    tiles = [p.reshape(-1, 8, p.shape[-1]) for p in parts]
    turned = [pltpu.roll(t, GROUP, 1) for t in tiles]
    low = lax.broadcasted_iota(jnp.int32, tiles[0].shape, 1) < GROUP
    even = jnp.concatenate(
        [jnp.where(low, tiles[0], turned[1]), jnp.where(low, tiles[2], turned[3])], axis=1
    )
    odd = jnp.concatenate(
        [jnp.where(low, turned[0], tiles[1]), jnp.where(low, turned[2], tiles[3])], axis=1
    )
    return even.astype(jnp.bfloat16), odd.astype(jnp.bfloat16)


def nt_dot(a, b):
    return lax.dot_general(a, b, (((1,), (1,)), ((), ())), preferred_element_type=jnp.float32)


def kernel(
    n, pair_hbm, mask_hbm, vec_refs, w_proj_hbm, w_gate_hbm, w_out_hbm, out_hbm,
    pair_v, mask_v, vec_v, w_proj_v, w_gate_v, w_out_v, out_v,
    send1, recv1, send2, recv2, stage, gate_v, col_v, in_sems, out_sem, sems,
):
    me = lax.axis_index("dap")
    rows, k, hidden = pair_v.shape[0], pair_v.shape[1], w_out_v.shape[0]
    half = n // 2

    def load(src, dst, i):
        copy = pltpu.make_async_copy(src, dst, in_sems.at[i])
        copy.start()
        return copy

    pair_in = load(pair_hbm, pair_v, 0)
    proj_in = load(w_proj_hbm, w_proj_v, 1)
    vec_in = [load(r, vec_v.at[pl.ds(i, 1)], 5 + i) for i, r in enumerate(vec_refs)]
    mask_in = load(mask_hbm, mask_v, 2)
    gate_in = load(w_gate_hbm, w_gate_v, 3)
    out_in = load(w_out_hbm, w_out_v, 4)

    barrier = pltpu.get_barrier_semaphore()

    @pl.loop(1, n)
    def _(s):
        pl.semaphore_signal(barrier, inc=1, device_id={"dap": lax.rem(me + s, n)}, device_id_type=MESH)

    proj_in.wait()
    w_t = w_proj_v[...].T
    pair_in.wait()
    for copy in vec_in:
        copy.wait()
    mask_in.wait()
    gain, bias = vec_v[0:1, :], vec_v[1:2, :]
    lefts, rights, normeds = [], [], []
    for r in range(rows):
        x = pair_v[r].astype(jnp.float32)
        centred = x - jnp.mean(x, axis=1, keepdims=True)
        var = jnp.mean(centred * centred, axis=1, keepdims=True)
        normed = (centred * lax.rsqrt(var + 1e-05) * gain + bias).astype(jnp.bfloat16)
        pair_v[r] = normed
        proj = nt_dot(w_t, normed)
        mask = mask_v[r : r + 1, :].astype(jnp.float32)
        lefts.append(sigmoid(proj[0:hidden]) * proj[hidden : 2 * hidden] * mask)
        rights.append(sigmoid(proj[2 * hidden : 3 * hidden]) * proj[3 * hidden : 4 * hidden] * mask)
    for side, parts in enumerate((lefts, rights)):
        even, odd = interleave(parts)
        send1[:, 0, side] = even
        send1[:, 1, side] = odd

    def exchange(send, recv, sem):
        @pl.loop(1, n)
        def _(s):
            to = lax.rem(me + s, n)
            pltpu.make_async_remote_copy(
                src_ref=send.at[to // 2, lax.rem(to, 2)],
                dst_ref=recv.at[me],
                send_sem=sems.at[2 * sem],
                recv_sem=sems.at[2 * sem + 1],
                device_id={"dap": to},
                device_id_type=MESH,
            ).start()

        recv[me] = send[me // 2, lax.rem(me, 2)]

    def wait_all(recv, i):
        span = recv.at[pl.ds(0, n - 1)]
        pltpu.make_async_copy(span, span, sems.at[i]).wait()

    pl.semaphore_wait(barrier, n - 1)
    exchange(send1, recv1, 0)

    gate_in.wait()
    for r in range(rows):
        gate_v[r] = sigmoid(jnp.dot(pair_v[r], w_gate_v[...], preferred_element_type=jnp.float32))
    for i in range(2):
        col_v[i] = jnp.broadcast_to(vec_v[2 + i : 3 + i, :], (hidden, hidden)).T
    out_in.wait()

    wait_all(recv1, 1)
    for side in range(2):
        stage[side] = recv1[:, side].astype(jnp.float32).reshape(n * 16, k)
    products = []
    for c in range(GROUP):
        left = stage[0, pl.ds(c, n * rows, stride=GROUP), :].astype(jnp.bfloat16)
        right = stage[1, pl.ds(c, n * rows, stride=GROUP), :].astype(jnp.bfloat16)
        products.append(nt_dot(left, right))
    even, odd = interleave(products)
    send2[:, 0] = even
    send2[:, 1] = odd
    exchange(send2, recv2, 1)
    wait_all(recv2, 3)

    stage[0] = recv2[...].astype(jnp.float32).reshape(n * 16, k)
    copies = []
    for r in range(rows):
        t = stage[0, pl.ds(r, hidden, stride=GROUP), :]
        centred = t - jnp.mean(t, axis=0, keepdims=True)
        var = jnp.mean(centred * centred, axis=0, keepdims=True)
        normed = (centred * lax.rsqrt(var + 1e-05) * col_v[0] + col_v[1]).astype(jnp.bfloat16)
        linear = lax.dot_general(
            normed, w_out_v[...], (((0,), (0,)), ((), ())), preferred_element_type=jnp.float32
        )
        out_v[r] = (gate_v[r] * linear).astype(jnp.bfloat16)
        copy = pltpu.make_async_copy(out_v.at[r], out_hbm.at[r], out_sem.at[r])
        copy.start()
        copies.append(copy)
    wait_all(recv1, 0)
    wait_all(recv2, 2)
    for copy in copies:
        copy.wait()


def fused(n, pair, pair_mask, ln_gain, ln_bias, w_proj, w_gate, tri_gain, tri_bias, w_out):
    rows, k, c = pair.shape
    hidden = w_out.shape[0]
    bf16, f32 = jnp.bfloat16, jnp.float32
    vecs = [v.reshape(1, -1) for v in (ln_gain, ln_bias, tri_gain, tri_bias)]
    any_spec = pl.BlockSpec(memory_space=pl.ANY)

    def run(pair_r, mask_r, g1, b1, g2, b2, wp, wg, wo, out_r, *scratch):
        kernel(n, pair_r, mask_r, (g1, b1, g2, b2), wp, wg, wo, out_r, *scratch)

    return pl.pallas_call(
        run,
        out_shape=jax.ShapeDtypeStruct((rows, k, c), bf16),
        in_specs=[any_spec] * 9,
        out_specs=any_spec,
        scratch_shapes=[
            pltpu.VMEM((rows, k, c), bf16),
            pltpu.VMEM((rows, k), jnp.int32),
            pltpu.VMEM((8, c), f32),
            pltpu.VMEM(w_proj.shape, bf16),
            pltpu.VMEM(w_gate.shape, bf16),
            pltpu.VMEM(w_out.shape, bf16),
            pltpu.VMEM((rows, k, c), bf16),
            pltpu.VMEM((n // 2, 2, 2, 16, k), bf16),
            pltpu.VMEM((n, 2, 16, k), bf16),
            pltpu.VMEM((n // 2, 2, 16, k), bf16),
            pltpu.VMEM((n, 16, k), bf16),
            pltpu.VMEM((2, n * 16, k), f32),
            pltpu.VMEM((rows, k, c), f32),
            pltpu.VMEM((2, hidden, k), f32),
            pltpu.SemaphoreType.DMA((9,)),
            pltpu.SemaphoreType.DMA((rows,)),
            pltpu.SemaphoreType.DMA((4,)),
        ],
        compiler_params=pltpu.CompilerParams(
            collective_id=0, has_side_effects=True, vmem_limit_bytes=16 * 2**20
        ),
    )(pair, pair_mask, *vecs, w_proj, w_gate, w_out)


def fits(mesh, pair, w_out):
    n = mesh.shape["dap"]
    rows, k, c = pair.shape
    return (
        mesh.shape["sub"] == 1
        and n % 4 == 0
        and rows == GROUP
        and w_out.shape[0] == GROUP * n
        and k == rows * n
        and c == k
        and k % 128 == 0
    )


def solution(mesh):
    placed = (
        P(("grp", "dap"), "sub", None),
        P(("grp", "dap"), "sub"),
        P(),
        P(),
        P(),
        P(),
        P(),
        P(),
        P(),
    )

    def local(pair, *rest):
        if fits(mesh, pair, rest[-1]):
            return fused(mesh.shape["dap"], pair, *rest)
        return body(pair, *rest)

    return jax.shard_map(
        local, mesh=mesh, in_specs=placed, out_specs=P(("grp", "dap"), "sub", None), check_vma=False
    )
```

```python
import functools

import jax
import jax.numpy as jnp
from jax import lax
from jax.experimental import pallas as pl
from jax.experimental.pallas import tpu as pltpu
from jax.sharding import PartitionSpec as P

MESH = pl.DeviceIdType.MESH
GROUP = 4


def layer_norm(values, gain, bias, axis):
    mean = jnp.mean(values, axis=axis, keepdims=True)
    var = jnp.mean((values - mean) ** 2, axis=axis, keepdims=True)
    return (values - mean) * lax.rsqrt(var + 1e-05) * gain + bias


def body(pair, pair_mask, ln_gain, ln_bias, w_proj, w_gate, tri_gain, tri_bias, w_out):
    hidden = w_out.shape[0]
    normed = layer_norm(pair.astype(jnp.float32), ln_gain, ln_bias, -1).astype(jnp.bfloat16)
    proj = jnp.einsum("rkc,cd->drk", normed, w_proj, preferred_element_type=jnp.float32)
    maskf = pair_mask.astype(jnp.float32)
    left = (jax.nn.sigmoid(proj[0:hidden]) * proj[hidden : 2 * hidden] * maskf).astype(jnp.bfloat16)
    right = (
        jax.nn.sigmoid(proj[2 * hidden : 3 * hidden]) * proj[3 * hidden : 4 * hidden] * maskf
    ).astype(jnp.bfloat16)
    left_all, right_all = (
        lax.all_to_all(left, "dap", split_axis=0, concat_axis=1, tiled=True),
        lax.all_to_all(right, "dap", split_axis=0, concat_axis=1, tiled=True),
    )
    out_gate = jax.nn.sigmoid(
        jnp.einsum("rjc,cd->rjd", normed, w_gate, preferred_element_type=jnp.float32)
    )
    partial_value = jnp.einsum(
        "hjk,hik->hij", right_all, left_all, preferred_element_type=jnp.float32
    ).astype(jnp.bfloat16)
    moved = lax.all_to_all(partial_value, "dap", split_axis=1, concat_axis=0, tiled=True)
    tri = lax.psum_scatter(
        moved.astype(jnp.float32).astype(jnp.bfloat16), "sub", scatter_dimension=2, tiled=True
    )
    tri_normed = layer_norm(
        tri.astype(jnp.float32), tri_gain[:, None, None], tri_bias[:, None, None], 0
    ).astype(jnp.bfloat16)
    linear = jnp.einsum("crj,cd->rjd", tri_normed, w_out, preferred_element_type=jnp.float32)
    return (out_gate * linear).astype(jnp.bfloat16)


def sigmoid(x):
    return 0.5 * jnp.tanh(0.5 * x) + 0.5


def interleave(parts):
    tiles = [p.reshape(-1, 8, p.shape[-1]) for p in parts]
    turned = [pltpu.roll(t, GROUP, 1) for t in tiles]
    low = lax.broadcasted_iota(jnp.int32, tiles[0].shape, 1) < GROUP
    even = jnp.concatenate(
        [jnp.where(low, tiles[0], turned[1]), jnp.where(low, tiles[2], turned[3])], axis=1
    )
    odd = jnp.concatenate(
        [jnp.where(low, turned[0], tiles[1]), jnp.where(low, turned[2], tiles[3])], axis=1
    )
    return even.astype(jnp.bfloat16), odd.astype(jnp.bfloat16)


def nt_dot(a, b):
    return lax.dot_general(a, b, (((1,), (1,)), ((), ())), preferred_element_type=jnp.float32)


def kernel(
    n, pair_hbm, mask_hbm, vec_refs, w_proj_hbm, w_gate_hbm, w_out_hbm, out_v,
    pair_v, mask_v, vec_v, w_proj_v, w_gate_v, w_out_v,
    send1, recv1, send2, recv2, stage, gate_v, col_v, in_sems, sems,
):
    me = lax.axis_index("dap")
    rows, k, hidden = pair_v.shape[0], pair_v.shape[1], w_out_v.shape[0]
    half = n // 2

    def load(src, dst, i):
        copy = pltpu.make_async_copy(src, dst, in_sems.at[i])
        copy.start()
        return copy

    pair_in = load(pair_hbm, pair_v, 0)
    proj_in = load(w_proj_hbm, w_proj_v, 1)
    vec_in = [load(r, vec_v.at[pl.ds(i, 1)], 5 + i) for i, r in enumerate(vec_refs)]
    mask_in = load(mask_hbm, mask_v, 2)
    gate_in = load(w_gate_hbm, w_gate_v, 3)
    out_in = load(w_out_hbm, w_out_v, 4)

    barrier = pltpu.get_barrier_semaphore()

    @pl.loop(1, n)
    def _(s):
        pl.semaphore_signal(barrier, inc=1, device_id={"dap": lax.rem(me + s, n)}, device_id_type=MESH)

    proj_in.wait()
    w_t = w_proj_v[...].T
    pair_in.wait()
    for copy in vec_in:
        copy.wait()
    mask_in.wait()
    gain, bias = vec_v[0:1, :], vec_v[1:2, :]
    lefts, rights, normeds = [], [], []
    for r in range(rows):
        x = pair_v[r].astype(jnp.float32)
        centred = x - jnp.mean(x, axis=1, keepdims=True)
        var = jnp.mean(centred * centred, axis=1, keepdims=True)
        normed = (centred * lax.rsqrt(var + 1e-05) * gain + bias).astype(jnp.bfloat16)
        pair_v[r] = normed
        proj = nt_dot(w_t, normed)
        mask = mask_v[r : r + 1, :].astype(jnp.float32)
        lefts.append(sigmoid(proj[0:hidden]) * proj[hidden : 2 * hidden] * mask)
        rights.append(sigmoid(proj[2 * hidden : 3 * hidden]) * proj[3 * hidden : 4 * hidden] * mask)
    for side, parts in enumerate((lefts, rights)):
        even, odd = interleave(parts)
        send1[:, 0, side] = even
        send1[:, 1, side] = odd

    def exchange(send, recv, sem):
        @pl.loop(1, n)
        def _(s):
            to = lax.rem(me + s, n)
            pltpu.make_async_remote_copy(
                src_ref=send.at[to // 2, lax.rem(to, 2)],
                dst_ref=recv.at[me],
                send_sem=sems.at[2 * sem],
                recv_sem=sems.at[2 * sem + 1],
                device_id={"dap": to},
                device_id_type=MESH,
            ).start()

        recv[me] = send[me // 2, lax.rem(me, 2)]

    def wait_all(recv, i):
        span = recv.at[pl.ds(0, n - 1)]
        pltpu.make_async_copy(span, span, sems.at[i]).wait()

    pl.semaphore_wait(barrier, n - 1)
    exchange(send1, recv1, 0)

    gate_in.wait()
    for r in range(rows):
        gate_v[r] = sigmoid(jnp.dot(pair_v[r], w_gate_v[...], preferred_element_type=jnp.float32))
    for i in range(2):
        col_v[i] = jnp.broadcast_to(vec_v[2 + i : 3 + i, :], (hidden, hidden)).T
    out_in.wait()

    wait_all(recv1, 1)
    for side in range(2):
        stage[side] = recv1[:, side].astype(jnp.float32).reshape(n * 16, k)
    products = []
    for c in range(GROUP):
        left = stage[0, pl.ds(c, n * rows, stride=GROUP), :].astype(jnp.bfloat16)
        right = stage[1, pl.ds(c, n * rows, stride=GROUP), :].astype(jnp.bfloat16)
        products.append(nt_dot(left, right))
    even, odd = interleave(products)
    send2[:, 0] = even
    send2[:, 1] = odd
    exchange(send2, recv2, 1)
    wait_all(recv2, 3)

    stage[0] = recv2[...].astype(jnp.float32).reshape(n * 16, k)
    for r in range(rows):
        t = stage[0, pl.ds(r, hidden, stride=GROUP), :]
        centred = t - jnp.mean(t, axis=0, keepdims=True)
        var = jnp.mean(centred * centred, axis=0, keepdims=True)
        normed = (centred * lax.rsqrt(var + 1e-05) * col_v[0] + col_v[1]).astype(jnp.bfloat16)
        linear = lax.dot_general(
            normed, w_out_v[...], (((0,), (0,)), ((), ())), preferred_element_type=jnp.float32
        )
        out_v[r] = (gate_v[r] * linear).astype(jnp.bfloat16)
    wait_all(recv1, 0)
    wait_all(recv2, 2)


def fused(n, pair, pair_mask, ln_gain, ln_bias, w_proj, w_gate, tri_gain, tri_bias, w_out):
    rows, k, c = pair.shape
    hidden = w_out.shape[0]
    bf16, f32 = jnp.bfloat16, jnp.float32
    vecs = [v.reshape(1, -1) for v in (ln_gain, ln_bias, tri_gain, tri_bias)]
    hbm_spec = pl.BlockSpec(memory_space=pltpu.HBM)

    def run(pair_r, mask_r, g1, b1, g2, b2, wp, wg, wo, out_r, *scratch):
        kernel(n, pair_r, mask_r, (g1, b1, g2, b2), wp, wg, wo, out_r, *scratch)

    return pl.pallas_call(
        run,
        out_shape=jax.ShapeDtypeStruct((rows, k, c), bf16),
        in_specs=[hbm_spec] * 9,
        out_specs=pl.BlockSpec(memory_space=pltpu.VMEM),
        scratch_shapes=[
            pltpu.VMEM((rows, k, c), bf16),
            pltpu.VMEM((rows, k), jnp.int32),
            pltpu.VMEM((8, c), f32),
            pltpu.VMEM(w_proj.shape, bf16),
            pltpu.VMEM(w_gate.shape, bf16),
            pltpu.VMEM(w_out.shape, bf16),
            pltpu.VMEM((n // 2, 2, 2, 16, k), bf16),
            pltpu.VMEM((n, 2, 16, k), bf16),
            pltpu.VMEM((n // 2, 2, 16, k), bf16),
            pltpu.VMEM((n, 16, k), bf16),
            pltpu.VMEM((2, n * 16, k), f32),
            pltpu.VMEM((rows, k, c), f32),
            pltpu.VMEM((2, hidden, k), f32),
            pltpu.SemaphoreType.DMA((9,)),
            pltpu.SemaphoreType.DMA((4,)),
        ],
        compiler_params=pltpu.CompilerParams(
            collective_id=0, has_side_effects=True, vmem_limit_bytes=16 * 2**20
        ),
    )(*[pltpu.with_memory_space_constraint(x, pltpu.HBM) for x in (pair, pair_mask, *vecs, w_proj, w_gate, w_out)])


def fits(mesh, pair, w_out):
    n = mesh.shape["dap"]
    rows, k, c = pair.shape
    return (
        mesh.shape["sub"] == 1
        and n % 4 == 0
        and rows == GROUP
        and w_out.shape[0] == GROUP * n
        and k == rows * n
        and c == k
        and k % 128 == 0
    )


def solution(mesh):
    placed = (
        P(("grp", "dap"), "sub", None),
        P(("grp", "dap"), "sub"),
        P(),
        P(),
        P(),
        P(),
        P(),
        P(),
        P(),
    )

    def local(pair, *rest):
        if fits(mesh, pair, rest[-1]):
            return fused(mesh.shape["dap"], pair, *rest)
        return body(pair, *rest)

    return jax.shard_map(
        local, mesh=mesh, in_specs=placed, out_specs=P(("grp", "dap"), "sub", None), check_vma=False
    )
```

```python
import functools

import jax
import jax.numpy as jnp
from jax import lax
from jax.experimental import pallas as pl
from jax.experimental.pallas import tpu as pltpu
from jax.sharding import PartitionSpec as P

MESH = pl.DeviceIdType.MESH
OWNED = 8


def layer_norm(values, gain, bias, axis):
    mean = jnp.mean(values, axis=axis, keepdims=True)
    var = jnp.mean((values - mean) ** 2, axis=axis, keepdims=True)
    return (values - mean) * lax.rsqrt(var + 1e-05) * gain + bias


def body(pair, pair_mask, ln_gain, ln_bias, w_proj, w_gate, tri_gain, tri_bias, w_out):
    hidden = w_out.shape[0]
    normed = layer_norm(pair.astype(jnp.float32), ln_gain, ln_bias, -1).astype(jnp.bfloat16)
    proj = jnp.einsum("rkc,cd->drk", normed, w_proj, preferred_element_type=jnp.float32)
    maskf = pair_mask.astype(jnp.float32)
    left = (jax.nn.sigmoid(proj[0:hidden]) * proj[hidden : 2 * hidden] * maskf).astype(jnp.bfloat16)
    right = (
        jax.nn.sigmoid(proj[2 * hidden : 3 * hidden]) * proj[3 * hidden : 4 * hidden] * maskf
    ).astype(jnp.bfloat16)
    left_all, right_all = (
        lax.all_to_all(left, "dap", split_axis=0, concat_axis=1, tiled=True),
        lax.all_to_all(right, "dap", split_axis=0, concat_axis=1, tiled=True),
    )
    out_gate = jax.nn.sigmoid(
        jnp.einsum("rjc,cd->rjd", normed, w_gate, preferred_element_type=jnp.float32)
    )
    partial_value = jnp.einsum(
        "hjk,hik->hij", right_all, left_all, preferred_element_type=jnp.float32
    ).astype(jnp.bfloat16)
    moved = lax.all_to_all(partial_value, "dap", split_axis=1, concat_axis=0, tiled=True)
    tri = lax.psum_scatter(
        moved.astype(jnp.float32).astype(jnp.bfloat16), "sub", scatter_dimension=2, tiled=True
    )
    tri_normed = layer_norm(
        tri.astype(jnp.float32), tri_gain[:, None, None], tri_bias[:, None, None], 0
    ).astype(jnp.bfloat16)
    linear = jnp.einsum("crj,cd->rjd", tri_normed, w_out, preferred_element_type=jnp.float32)
    return (out_gate * linear).astype(jnp.bfloat16)


def sigmoid(x):
    return 0.5 * jnp.tanh(0.5 * x) + 0.5


def nt_dot(a, b):
    return lax.dot_general(a, b, (((1,), (1,)), ((), ())), preferred_element_type=jnp.float32)


def kernel(
    n, pair_hbm, mask_hbm, vec_refs, w_proj_hbm, w_gate_hbm, w_out_hbm, out_v,
    pair_v, mask_v, vec_v, w_proj_v, w_gate_v, w_out_v,
    send_r, recv_r, send_l, recv_l, send_t, recv_t, stage, gate_v, col_v,
    in_sems, r_sems, l_sems, t_sems,
):
    me = lax.axis_index("dap")
    rows, k, hidden = pair_v.shape[0], pair_v.shape[1], w_out_v.shape[0]
    half = n // 2
    base, place = me // half * half, lax.rem(me, half)

    def load(src, dst, i):
        copy = pltpu.make_async_copy(src, dst, in_sems.at[i])
        copy.start()
        return copy

    def each_other(act):
        @pl.loop(0, half)
        def _(s):
            to = lax.rem(place + s, half)
            act(half - base + to, to)

    def each_own(act):
        @pl.loop(1, half)
        def _(s):
            to = lax.rem(place + s, half)
            act(base + to, to)

    def greet(to, _):
        pl.semaphore_signal(barrier, inc=1, device_id={"dap": to}, device_id_type=MESH)

    barrier = pltpu.get_barrier_semaphore()
    pair_in = load(pair_hbm, pair_v, 0)
    proj_in = load(w_proj_hbm, w_proj_v, 1)
    each_other(greet)
    each_own(greet)
    vec_in = [load(r, vec_v.at[pl.ds(i, 1)], 5 + i) for i, r in enumerate(vec_refs)]
    mask_in = load(mask_hbm, mask_v, 2)
    gate_in = load(w_gate_hbm, w_gate_v, 3)
    out_in = load(w_out_hbm, w_out_v, 4)

    def sender(send, recv, slot, sems):
        def act(to, to_place):
            pltpu.make_async_remote_copy(
                src_ref=send.at[to_place],
                dst_ref=recv.at[slot],
                send_sem=sems.at[0],
                recv_sem=sems.at[1],
                device_id={"dap": to},
                device_id_type=MESH,
            ).start()

        return act

    def wait_blocks(recv, sem, count):
        span = recv.at[pl.ds(0, count)]
        pltpu.make_async_copy(span, span, sem).wait()

    proj_in.wait()
    w_t = w_proj_v[...].T
    pair_in.wait()
    for copy in vec_in:
        copy.wait()
    mask_in.wait()
    gain, bias = vec_v[0:1, :], vec_v[1:2, :]

    def edge(proj, mask):
        return sigmoid(proj[0:hidden]) * proj[hidden : 2 * hidden] * mask

    lefts, rights = [], []
    for r in range(rows):
        x = pair_v[r].astype(jnp.float32)
        centred = x - jnp.mean(x, axis=1, keepdims=True)
        var = jnp.mean(centred * centred, axis=1, keepdims=True)
        normed = (centred * lax.rsqrt(var + 1e-05) * gain + bias).astype(jnp.bfloat16)
        pair_v[r] = normed
        proj = nt_dot(w_t, normed)
        mask = mask_v[r : r + 1, :].astype(jnp.float32)
        lefts.append(edge(proj[0 : 2 * hidden], mask).reshape(half, OWNED, k))
        rights.append(edge(proj[2 * hidden : 4 * hidden], mask).reshape(half, OWNED, k))
    send_r[...] = jnp.concatenate(rights, axis=1).astype(jnp.bfloat16)
    send_l[...] = jnp.concatenate(lefts, axis=1).astype(jnp.bfloat16)
    pl.semaphore_wait(barrier, n - 1)
    each_other(sender(send_r, recv_r, me, r_sems))
    each_own(sender(send_r, recv_r, me, r_sems))
    each_own(sender(send_l, recv_l, place, l_sems))
    recv_r[me] = send_r[place]
    recv_l[place] = send_l[place]

    gate_in.wait()
    for r in range(rows):
        gate_v[r] = sigmoid(jnp.dot(pair_v[r], w_gate_v[...], preferred_element_type=jnp.float32))
    for i in range(2):
        col_v[i] = jnp.broadcast_to(vec_v[2 + i : 3 + i, :], (k, hidden)).T
    out_in.wait()

    ours = half * rows
    wait_blocks(recv_l, l_sems.at[1], half - 1)
    lefts = []
    area = stage.at[pl.ds(0, ours * OWNED)]
    area[...] = recv_l[...].astype(jnp.float32).reshape(ours * OWNED, k)
    for c in range(OWNED):
        lefts.append(area[pl.ds(c, ours, stride=OWNED), :].astype(jnp.bfloat16))
    wait_blocks(recv_r, r_sems.at[1], n - 1)
    stage[...] = recv_r[...].astype(jnp.float32).reshape(n * rows * OWNED, k)
    products = []
    for c in range(OWNED):
        right = stage[pl.ds(c, n * rows, stride=OWNED), :].astype(jnp.bfloat16)
        products.append(nt_dot(lefts[c], right))
    for c in range(OWNED):
        area[pl.ds(c, ours, stride=OWNED), :] = products[c]
    send_t[...] = area[...].astype(jnp.bfloat16).reshape(half, rows * OWNED, k)
    each_own(sender(send_t, recv_t, place, t_sems))
    recv_t[place] = send_t[place]

    wait_blocks(recv_t, t_sems.at[1], half - 1)
    tri = recv_t[...].astype(jnp.float32)
    for r in range(rows):
        t = tri[:, r * OWNED : (r + 1) * OWNED].reshape(hidden, k)
        centred = t - jnp.mean(t, axis=0, keepdims=True)
        var = jnp.mean(centred * centred, axis=0, keepdims=True)
        normed = (centred * lax.rsqrt(var + 1e-05) * col_v[0] + col_v[1]).astype(jnp.bfloat16)
        linear = lax.dot_general(
            normed, w_out_v[...], (((0,), (0,)), ((), ())), preferred_element_type=jnp.float32
        )
        out_v[r] = (gate_v[r] * linear).astype(jnp.bfloat16)
    wait_blocks(recv_r, r_sems.at[0], n - 1)
    wait_blocks(recv_l, l_sems.at[0], half - 1)
    wait_blocks(recv_t, t_sems.at[0], half - 1)


def fused(n, pair, pair_mask, ln_gain, ln_bias, w_proj, w_gate, tri_gain, tri_bias, w_out):
    rows, k, c = pair.shape
    hidden = w_out.shape[0]
    bf16, f32 = jnp.bfloat16, jnp.float32
    vecs = [v.reshape(1, -1) for v in (ln_gain, ln_bias, tri_gain, tri_bias)]
    hbm_spec = pl.BlockSpec(memory_space=pltpu.HBM)

    def run(pair_r, mask_r, g1, b1, g2, b2, wp, wg, wo, out_r, *scratch):
        kernel(n, pair_r, mask_r, (g1, b1, g2, b2), wp, wg, wo, out_r, *scratch)

    return pl.pallas_call(
        run,
        out_shape=jax.ShapeDtypeStruct((rows, k, c), bf16),
        in_specs=[hbm_spec] * 9,
        out_specs=pl.BlockSpec(memory_space=pltpu.VMEM),
        scratch_shapes=[
            pltpu.VMEM((rows, k, c), bf16),
            pltpu.VMEM((rows, k), jnp.int32),
            pltpu.VMEM((8, c), f32),
            pltpu.VMEM(w_proj.shape, bf16),
            pltpu.VMEM(w_gate.shape, bf16),
            pltpu.VMEM(w_out.shape, bf16),
            *[
                pltpu.VMEM((blocks, rows * OWNED, k), bf16)
                for blocks in (n // 2, n, n // 2, n // 2, n // 2, n // 2)
            ],
            pltpu.VMEM((n * rows * OWNED, k), f32),
            pltpu.VMEM((rows, k, c), f32),
            pltpu.VMEM((2, hidden, k), f32),
            pltpu.SemaphoreType.DMA((9,)),
            pltpu.SemaphoreType.DMA((2,)),
            pltpu.SemaphoreType.DMA((2,)),
            pltpu.SemaphoreType.DMA((2,)),
        ],
        compiler_params=pltpu.CompilerParams(
            collective_id=0, has_side_effects=True, vmem_limit_bytes=16 * 2**20
        ),
    )(*[pltpu.with_memory_space_constraint(x, pltpu.HBM) for x in (pair, pair_mask, *vecs, w_proj, w_gate, w_out)])


def fits(mesh, pair, w_out):
    n = mesh.shape["dap"]
    rows, k, c = pair.shape
    hidden = w_out.shape[0]
    return (
        mesh.shape["sub"] == 1
        and n % 2 == 0
        and 2 * hidden == OWNED * n
        and rows * OWNED % 16 == 0
        and k == rows * n
        and k % 128 == 0
        and c == hidden
        and c % 128 == 0
    )


def solution(mesh):
    placed = (
        P(("grp", "dap"), "sub", None),
        P(("grp", "dap"), "sub"),
        P(),
        P(),
        P(),
        P(),
        P(),
        P(),
        P(),
    )

    def local(pair, *rest):
        if fits(mesh, pair, rest[-1]):
            return fused(mesh.shape["dap"], pair, *rest)
        return body(pair, *rest)

    return jax.shard_map(
        local, mesh=mesh, in_specs=placed, out_specs=P(("grp", "dap"), "sub", None), check_vma=False
    )
```

```python
import functools

import jax
import jax.numpy as jnp
from jax import lax
from jax.experimental import pallas as pl
from jax.experimental.pallas import tpu as pltpu
from jax.sharding import PartitionSpec as P

MESH = pl.DeviceIdType.MESH
OWNED = 8


def layer_norm(values, gain, bias, axis):
    mean = jnp.mean(values, axis=axis, keepdims=True)
    var = jnp.mean((values - mean) ** 2, axis=axis, keepdims=True)
    return (values - mean) * lax.rsqrt(var + 1e-05) * gain + bias


def body(pair, pair_mask, ln_gain, ln_bias, w_proj, w_gate, tri_gain, tri_bias, w_out):
    hidden = w_out.shape[0]
    normed = layer_norm(pair.astype(jnp.float32), ln_gain, ln_bias, -1).astype(jnp.bfloat16)
    proj = jnp.einsum("rkc,cd->drk", normed, w_proj, preferred_element_type=jnp.float32)
    maskf = pair_mask.astype(jnp.float32)
    left = (jax.nn.sigmoid(proj[0:hidden]) * proj[hidden : 2 * hidden] * maskf).astype(jnp.bfloat16)
    right = (
        jax.nn.sigmoid(proj[2 * hidden : 3 * hidden]) * proj[3 * hidden : 4 * hidden] * maskf
    ).astype(jnp.bfloat16)
    left_all, right_all = (
        lax.all_to_all(left, "dap", split_axis=0, concat_axis=1, tiled=True),
        lax.all_to_all(right, "dap", split_axis=0, concat_axis=1, tiled=True),
    )
    out_gate = jax.nn.sigmoid(
        jnp.einsum("rjc,cd->rjd", normed, w_gate, preferred_element_type=jnp.float32)
    )
    partial_value = jnp.einsum(
        "hjk,hik->hij", right_all, left_all, preferred_element_type=jnp.float32
    ).astype(jnp.bfloat16)
    moved = lax.all_to_all(partial_value, "dap", split_axis=1, concat_axis=0, tiled=True)
    tri = lax.psum_scatter(
        moved.astype(jnp.float32).astype(jnp.bfloat16), "sub", scatter_dimension=2, tiled=True
    )
    tri_normed = layer_norm(
        tri.astype(jnp.float32), tri_gain[:, None, None], tri_bias[:, None, None], 0
    ).astype(jnp.bfloat16)
    linear = jnp.einsum("crj,cd->rjd", tri_normed, w_out, preferred_element_type=jnp.float32)
    return (out_gate * linear).astype(jnp.bfloat16)


def sigmoid(x):
    return 0.5 * jnp.tanh(0.5 * x) + 0.5


def nt_dot(a, b):
    return lax.dot_general(a, b, (((1,), (1,)), ((), ())), preferred_element_type=jnp.float32)


def kernel(
    n, pair_hbm, mask_hbm, vec_refs, w_proj_hbm, w_gate_hbm, w_out_hbm, out_v,
    pair_v, mask_v, vec_v, w_proj_v, w_gate_v, w_out_v,
    send_r, recv_r, send_l, recv_l, send_t, recv_t, stage, gate_v, col_v,
    in_sems, r_sems, l_sems, t_sems,
):
    me = lax.axis_index("dap")
    rows, k, hidden = pair_v.shape[0], pair_v.shape[1], w_out_v.shape[0]
    half = n // 2
    base, place = me // half * half, lax.rem(me, half)

    def load(src, dst, i):
        copy = pltpu.make_async_copy(src, dst, in_sems.at[i])
        copy.start()
        return copy

    def each_other(act):
        @pl.loop(0, half)
        def _(s):
            to = lax.rem(place + s, half)
            act(half - base + to, to)

    def each_own(act):
        @pl.loop(1, half)
        def _(s):
            to = lax.rem(place + s, half)
            act(base + to, to)

    def greet(to, _):
        pl.semaphore_signal(barrier, inc=1, device_id={"dap": to}, device_id_type=MESH)

    barrier = pltpu.get_barrier_semaphore()
    pair_in = load(pair_hbm, pair_v, 0)
    proj_in = load(w_proj_hbm, w_proj_v, 1)
    each_other(greet)
    each_own(greet)
    vec_in = [load(r, vec_v.at[pl.ds(i, 1)], 5 + i) for i, r in enumerate(vec_refs)]
    mask_in = load(mask_hbm, mask_v, 2)
    gate_in = load(w_gate_hbm, w_gate_v, 3)
    out_in = load(w_out_hbm, w_out_v, 4)

    def sender(send, recv, slot, sems):
        def act(to, to_place):
            pltpu.make_async_remote_copy(
                src_ref=send.at[to_place],
                dst_ref=recv.at[slot],
                send_sem=sems.at[0],
                recv_sem=sems.at[1],
                device_id={"dap": to},
                device_id_type=MESH,
            ).start()

        return act

    def wait_blocks(recv, sem, count):
        span = recv.at[pl.ds(0, count)]
        pltpu.make_async_copy(span, span, sem).wait()

    proj_in.wait()
    w_t = w_proj_v[...].T
    pair_in.wait()
    for copy in vec_in:
        copy.wait()
    mask_in.wait()
    gain, bias = vec_v[0:1, :], vec_v[1:2, :]

    def edge(proj, mask):
        return sigmoid(proj[0:hidden]) * proj[hidden : 2 * hidden] * mask

    lefts, rights = [], []
    for r in range(rows):
        x = pair_v[r].astype(jnp.float32)
        centred = x - jnp.mean(x, axis=1, keepdims=True)
        var = jnp.mean(centred * centred, axis=1, keepdims=True)
        normed = (centred * lax.rsqrt(var + 1e-05) * gain + bias).astype(jnp.bfloat16)
        pair_v[r] = normed
        proj = nt_dot(w_t, normed)
        mask = mask_v[r : r + 1, :].astype(jnp.float32)
        lefts.append(edge(proj[0 : 2 * hidden], mask).reshape(half, OWNED, k))
        rights.append(edge(proj[2 * hidden : 4 * hidden], mask).reshape(half, OWNED, k))
    send_r[...] = jnp.concatenate(rights, axis=1).astype(jnp.bfloat16)
    send_l[...] = jnp.concatenate(lefts, axis=1).astype(jnp.bfloat16)
    pl.semaphore_wait(barrier, n - 1)
    each_own(sender(send_l, recv_l, place, l_sems))
    each_own(sender(send_r, recv_r, me, r_sems))
    each_other(sender(send_r, recv_r, me, r_sems))
    recv_r[me] = send_r[place]
    recv_l[place] = send_l[place]

    gate_in.wait()
    for r in range(rows):
        gate_v[r] = sigmoid(jnp.dot(pair_v[r], w_gate_v[...], preferred_element_type=jnp.float32))
    for i in range(2):
        col_v[i] = jnp.broadcast_to(vec_v[2 + i : 3 + i, :], (k, hidden)).T
    out_in.wait()

    ours = half * rows
    wait_blocks(recv_l, l_sems.at[1], half - 1)
    lefts = []
    area = stage.at[pl.ds(0, ours * OWNED)]
    area[...] = recv_l[...].astype(jnp.float32).reshape(ours * OWNED, k)
    for c in range(OWNED):
        lefts.append(area[pl.ds(c, ours, stride=OWNED), :].astype(jnp.bfloat16))
    wait_blocks(recv_r, r_sems.at[1], n - 1)
    stage[...] = recv_r[...].astype(jnp.float32).reshape(n * rows * OWNED, k)
    products = []
    for c in range(OWNED):
        right = stage[pl.ds(c, n * rows, stride=OWNED), :].astype(jnp.bfloat16)
        products.append(nt_dot(lefts[c], right))
    for c in range(OWNED):
        area[pl.ds(c, ours, stride=OWNED), :] = products[c]
    send_t[...] = area[...].astype(jnp.bfloat16).reshape(half, rows * OWNED, k)
    each_own(sender(send_t, recv_t, place, t_sems))
    recv_t[place] = send_t[place]

    wait_blocks(recv_t, t_sems.at[1], half - 1)
    tri = recv_t[...].astype(jnp.float32)
    for r in range(rows):
        t = tri[:, r * OWNED : (r + 1) * OWNED].reshape(hidden, k)
        centred = t - jnp.mean(t, axis=0, keepdims=True)
        var = jnp.mean(centred * centred, axis=0, keepdims=True)
        normed = (centred * lax.rsqrt(var + 1e-05) * col_v[0] + col_v[1]).astype(jnp.bfloat16)
        linear = lax.dot_general(
            normed, w_out_v[...], (((0,), (0,)), ((), ())), preferred_element_type=jnp.float32
        )
        out_v[r] = (gate_v[r] * linear).astype(jnp.bfloat16)
    wait_blocks(recv_r, r_sems.at[0], n - 1)
    wait_blocks(recv_l, l_sems.at[0], half - 1)
    wait_blocks(recv_t, t_sems.at[0], half - 1)


def fused(n, pair, pair_mask, ln_gain, ln_bias, w_proj, w_gate, tri_gain, tri_bias, w_out):
    rows, k, c = pair.shape
    hidden = w_out.shape[0]
    bf16, f32 = jnp.bfloat16, jnp.float32
    vecs = [v.reshape(1, -1) for v in (ln_gain, ln_bias, tri_gain, tri_bias)]
    hbm_spec = pl.BlockSpec(memory_space=pltpu.HBM)

    def run(pair_r, mask_r, g1, b1, g2, b2, wp, wg, wo, out_r, *scratch):
        kernel(n, pair_r, mask_r, (g1, b1, g2, b2), wp, wg, wo, out_r, *scratch)

    return pl.pallas_call(
        run,
        out_shape=jax.ShapeDtypeStruct((rows, k, c), bf16),
        in_specs=[hbm_spec] * 9,
        out_specs=pl.BlockSpec(memory_space=pltpu.VMEM),
        scratch_shapes=[
            pltpu.VMEM((rows, k, c), bf16),
            pltpu.VMEM((rows, k), jnp.int32),
            pltpu.VMEM((8, c), f32),
            pltpu.VMEM(w_proj.shape, bf16),
            pltpu.VMEM(w_gate.shape, bf16),
            pltpu.VMEM(w_out.shape, bf16),
            *[
                pltpu.VMEM((blocks, rows * OWNED, k), bf16)
                for blocks in (n // 2, n, n // 2, n // 2, n // 2, n // 2)
            ],
            pltpu.VMEM((n * rows * OWNED, k), f32),
            pltpu.VMEM((rows, k, c), f32),
            pltpu.VMEM((2, hidden, k), f32),
            pltpu.SemaphoreType.DMA((9,)),
            pltpu.SemaphoreType.DMA((2,)),
            pltpu.SemaphoreType.DMA((2,)),
            pltpu.SemaphoreType.DMA((2,)),
        ],
        compiler_params=pltpu.CompilerParams(
            collective_id=0, has_side_effects=True, vmem_limit_bytes=16 * 2**20
        ),
    )(*[pltpu.with_memory_space_constraint(x, pltpu.HBM) for x in (pair, pair_mask, *vecs, w_proj, w_gate, w_out)])


def fits(mesh, pair, w_out):
    n = mesh.shape["dap"]
    rows, k, c = pair.shape
    hidden = w_out.shape[0]
    return (
        mesh.shape["sub"] == 1
        and n % 2 == 0
        and 2 * hidden == OWNED * n
        and rows * OWNED % 16 == 0
        and k == rows * n
        and k % 128 == 0
        and c == hidden
        and c % 128 == 0
    )


def solution(mesh):
    placed = (
        P(("grp", "dap"), "sub", None),
        P(("grp", "dap"), "sub"),
        P(),
        P(),
        P(),
        P(),
        P(),
        P(),
        P(),
    )

    def local(pair, *rest):
        if fits(mesh, pair, rest[-1]):
            return fused(mesh.shape["dap"], pair, *rest)
        return body(pair, *rest)

    return jax.shard_map(
        local, mesh=mesh, in_specs=placed, out_specs=P(("grp", "dap"), "sub", None), check_vma=False
    )
```

```python
import functools

import jax
import jax.numpy as jnp
from jax import lax
from jax.experimental import pallas as pl
from jax.experimental.pallas import tpu as pltpu
from jax.sharding import PartitionSpec as P

MESH = pl.DeviceIdType.MESH
OWNED = 8


def layer_norm(values, gain, bias, axis):
    mean = jnp.mean(values, axis=axis, keepdims=True)
    var = jnp.mean((values - mean) ** 2, axis=axis, keepdims=True)
    return (values - mean) * lax.rsqrt(var + 1e-05) * gain + bias


def body(pair, pair_mask, ln_gain, ln_bias, w_proj, w_gate, tri_gain, tri_bias, w_out):
    hidden = w_out.shape[0]
    normed = layer_norm(pair.astype(jnp.float32), ln_gain, ln_bias, -1).astype(jnp.bfloat16)
    proj = jnp.einsum("rkc,cd->drk", normed, w_proj, preferred_element_type=jnp.float32)
    maskf = pair_mask.astype(jnp.float32)
    left = (jax.nn.sigmoid(proj[0:hidden]) * proj[hidden : 2 * hidden] * maskf).astype(jnp.bfloat16)
    right = (
        jax.nn.sigmoid(proj[2 * hidden : 3 * hidden]) * proj[3 * hidden : 4 * hidden] * maskf
    ).astype(jnp.bfloat16)
    left_all, right_all = (
        lax.all_to_all(left, "dap", split_axis=0, concat_axis=1, tiled=True),
        lax.all_to_all(right, "dap", split_axis=0, concat_axis=1, tiled=True),
    )
    out_gate = jax.nn.sigmoid(
        jnp.einsum("rjc,cd->rjd", normed, w_gate, preferred_element_type=jnp.float32)
    )
    partial_value = jnp.einsum(
        "hjk,hik->hij", right_all, left_all, preferred_element_type=jnp.float32
    ).astype(jnp.bfloat16)
    moved = lax.all_to_all(partial_value, "dap", split_axis=1, concat_axis=0, tiled=True)
    tri = lax.psum_scatter(
        moved.astype(jnp.float32).astype(jnp.bfloat16), "sub", scatter_dimension=2, tiled=True
    )
    tri_normed = layer_norm(
        tri.astype(jnp.float32), tri_gain[:, None, None], tri_bias[:, None, None], 0
    ).astype(jnp.bfloat16)
    linear = jnp.einsum("crj,cd->rjd", tri_normed, w_out, preferred_element_type=jnp.float32)
    return (out_gate * linear).astype(jnp.bfloat16)


def sigmoid(x):
    return 0.5 * jnp.tanh(0.5 * x) + 0.5


def nt_dot(a, b):
    return lax.dot_general(a, b, (((1,), (1,)), ((), ())), preferred_element_type=jnp.float32)


def kernel(
    n, pair_hbm, mask_hbm, vec_refs, w_proj_hbm, w_gate_hbm, w_out_hbm, out_v,
    pair_v, mask_v, vec_v, w_proj_v, w_gate_v, w_out_v,
    send_r, recv_r, send_l, recv_l, send_t, recv_t, stage, gate_v, col_v,
    in_sems, r_sems, l_sems, t_sems,
):
    me = lax.axis_index("dap")
    rows, k, hidden = pair_v.shape[0], pair_v.shape[1], w_out_v.shape[0]
    half = n // 2
    base, place = me // half * half, lax.rem(me, half)

    def load(src, dst, i):
        copy = pltpu.make_async_copy(src, dst, in_sems.at[i])
        copy.start()
        return copy

    def each_other(act):
        @pl.loop(0, half)
        def _(s):
            to = lax.rem(place + s, half)
            act(half - base + to, to)

    def each_own(act):
        @pl.loop(1, half)
        def _(s):
            to = lax.rem(place + s, half)
            act(base + to, to)

    def greet(to, _):
        pl.semaphore_signal(barrier, inc=1, device_id={"dap": to}, device_id_type=MESH)

    barrier = pltpu.get_barrier_semaphore()
    pair_in = load(pair_hbm, pair_v, 0)
    proj_in = load(w_proj_hbm, w_proj_v, 1)
    each_other(greet)
    each_own(greet)
    vec_in = [load(r, vec_v.at[pl.ds(i, 1)], 5 + i) for i, r in enumerate(vec_refs)]
    mask_in = load(mask_hbm, mask_v, 2)
    gate_in = load(w_gate_hbm, w_gate_v, 3)
    out_in = load(w_out_hbm, w_out_v, 4)

    def sender(send, recv, slot, sems):
        def act(to, to_place):
            pltpu.make_async_remote_copy(
                src_ref=send.at[to_place],
                dst_ref=recv.at[slot],
                send_sem=sems.at[0],
                recv_sem=sems.at[1],
                device_id={"dap": to},
                device_id_type=MESH,
            ).start()

        return act

    def wait_blocks(recv, sem, count):
        span = recv.at[pl.ds(0, count)]
        pltpu.make_async_copy(span, span, sem).wait()

    proj_in.wait()
    w_t = w_proj_v[...].T
    pair_in.wait()
    for copy in vec_in:
        copy.wait()
    mask_in.wait()
    gain, bias = vec_v[0:1, :], vec_v[1:2, :]

    def edge(proj, mask):
        return sigmoid(proj[0:hidden]) * proj[hidden : 2 * hidden] * mask

    lefts, rights = [], []
    for r in range(rows):
        x = pair_v[r].astype(jnp.float32)
        centred = x - jnp.mean(x, axis=1, keepdims=True)
        var = jnp.mean(centred * centred, axis=1, keepdims=True)
        normed = (centred * lax.rsqrt(var + 1e-05) * gain + bias).astype(jnp.bfloat16)
        pair_v[r] = normed
        proj = nt_dot(w_t, normed)
        mask = mask_v[r : r + 1, :].astype(jnp.float32)
        lefts.append(edge(proj[0 : 2 * hidden], mask).reshape(half, OWNED, k))
        rights.append(edge(proj[2 * hidden : 4 * hidden], mask).reshape(half, OWNED, k))
    send_r[...] = jnp.concatenate(rights, axis=1).astype(jnp.bfloat16)
    send_l[...] = jnp.concatenate(lefts, axis=1).astype(jnp.bfloat16)
    pl.semaphore_wait(barrier, n - 1)
    each_own(sender(send_l, recv_l, place, l_sems))
    each_own(sender(send_r, recv_r, me, r_sems))
    each_other(sender(send_r, recv_r, me, r_sems))
    recv_r[me] = send_r[place]
    recv_l[place] = send_l[place]

    gate_in.wait()
    for r in range(rows):
        gate_v[r] = sigmoid(jnp.dot(pair_v[r], w_gate_v[...], preferred_element_type=jnp.float32))
    for i in range(2):
        col_v[i] = jnp.broadcast_to(vec_v[2 + i : 3 + i, :], (k, hidden)).T
    out_in.wait()

    ours = half * rows
    wait_blocks(recv_l, l_sems.at[1], half - 1)
    lefts = []
    area = stage.at[pl.ds(0, ours * OWNED)]
    area[...] = recv_l[...].astype(jnp.float32).reshape(ours * OWNED, k)
    for c in range(OWNED):
        lefts.append(area[pl.ds(c, ours, stride=OWNED), :].astype(jnp.bfloat16))
    wait_blocks(recv_r, r_sems.at[1], n - 1)
    stage[...] = recv_r[...].astype(jnp.float32).reshape(n * rows * OWNED, k)
    rights = [stage[pl.ds(c, n * rows, stride=OWNED), :].astype(jnp.bfloat16) for c in range(OWNED)]
    for part in range(2):
        few, first = ours // 2, part * (half // 2)
        for c in range(OWNED):
            area[pl.ds(part * few * OWNED + c, few, stride=OWNED), :] = nt_dot(lefts[c][part * few : (part + 1) * few], rights[c])
        send_t[pl.ds(first, half // 2)] = (
            area[pl.ds(part * few * OWNED, few * OWNED), :].astype(jnp.bfloat16).reshape(half // 2, rows * OWNED, k)
        )

        @pl.loop(0, half // 2)
        def _(s):
            to = first + lax.rem(place + s, half // 2)

            @pl.when(to != place)
            def _():
                sender(send_t, recv_t, place, t_sems)(base + to, to)

    recv_t[place] = send_t[place]

    wait_blocks(recv_t, t_sems.at[1], half - 1)
    tri = recv_t[...].astype(jnp.float32)
    for r in range(rows):
        t = tri[:, r * OWNED : (r + 1) * OWNED].reshape(hidden, k)
        centred = t - jnp.mean(t, axis=0, keepdims=True)
        var = jnp.mean(centred * centred, axis=0, keepdims=True)
        normed = (centred * lax.rsqrt(var + 1e-05) * col_v[0] + col_v[1]).astype(jnp.bfloat16)
        linear = lax.dot_general(
            normed, w_out_v[...], (((0,), (0,)), ((), ())), preferred_element_type=jnp.float32
        )
        out_v[r] = (gate_v[r] * linear).astype(jnp.bfloat16)
    wait_blocks(recv_r, r_sems.at[0], n - 1)
    wait_blocks(recv_l, l_sems.at[0], half - 1)
    wait_blocks(recv_t, t_sems.at[0], half - 1)


def fused(n, pair, pair_mask, ln_gain, ln_bias, w_proj, w_gate, tri_gain, tri_bias, w_out):
    rows, k, c = pair.shape
    hidden = w_out.shape[0]
    bf16, f32 = jnp.bfloat16, jnp.float32
    vecs = [v.reshape(1, -1) for v in (ln_gain, ln_bias, tri_gain, tri_bias)]
    hbm_spec = pl.BlockSpec(memory_space=pltpu.HBM)

    def run(pair_r, mask_r, g1, b1, g2, b2, wp, wg, wo, out_r, *scratch):
        kernel(n, pair_r, mask_r, (g1, b1, g2, b2), wp, wg, wo, out_r, *scratch)

    return pl.pallas_call(
        run,
        out_shape=jax.ShapeDtypeStruct((rows, k, c), bf16),
        in_specs=[hbm_spec] * 9,
        out_specs=pl.BlockSpec(memory_space=pltpu.VMEM),
        scratch_shapes=[
            pltpu.VMEM((rows, k, c), bf16),
            pltpu.VMEM((rows, k), jnp.int32),
            pltpu.VMEM((8, c), f32),
            pltpu.VMEM(w_proj.shape, bf16),
            pltpu.VMEM(w_gate.shape, bf16),
            pltpu.VMEM(w_out.shape, bf16),
            *[
                pltpu.VMEM((blocks, rows * OWNED, k), bf16)
                for blocks in (n // 2, n, n // 2, n // 2, n // 2, n // 2)
            ],
            pltpu.VMEM((n * rows * OWNED, k), f32),
            pltpu.VMEM((rows, k, c), f32),
            pltpu.VMEM((2, hidden, k), f32),
            pltpu.SemaphoreType.DMA((9,)),
            pltpu.SemaphoreType.DMA((2,)),
            pltpu.SemaphoreType.DMA((2,)),
            pltpu.SemaphoreType.DMA((2,)),
        ],
        compiler_params=pltpu.CompilerParams(
            collective_id=0, has_side_effects=True, vmem_limit_bytes=16 * 2**20
        ),
    )(*[pltpu.with_memory_space_constraint(x, pltpu.HBM) for x in (pair, pair_mask, *vecs, w_proj, w_gate, w_out)])


def fits(mesh, pair, w_out):
    n = mesh.shape["dap"]
    rows, k, c = pair.shape
    hidden = w_out.shape[0]
    return (
        mesh.shape["sub"] == 1
        and n % 4 == 0
        and 2 * hidden == OWNED * n
        and rows * OWNED % 16 == 0
        and k == rows * n
        and k % 128 == 0
        and c == hidden
        and c % 128 == 0
    )


def solution(mesh):
    placed = (
        P(("grp", "dap"), "sub", None),
        P(("grp", "dap"), "sub"),
        P(),
        P(),
        P(),
        P(),
        P(),
        P(),
        P(),
    )

    def local(pair, *rest):
        if fits(mesh, pair, rest[-1]):
            return fused(mesh.shape["dap"], pair, *rest)
        return body(pair, *rest)

    return jax.shard_map(
        local, mesh=mesh, in_specs=placed, out_specs=P(("grp", "dap"), "sub", None), check_vma=False
    )
```

```python
import functools

import jax
import jax.numpy as jnp
from jax import lax
from jax.experimental import pallas as pl
from jax.experimental.pallas import tpu as pltpu
from jax.sharding import PartitionSpec as P

MESH = pl.DeviceIdType.MESH
OWNED = 8


def layer_norm(values, gain, bias, axis):
    mean = jnp.mean(values, axis=axis, keepdims=True)
    var = jnp.mean((values - mean) ** 2, axis=axis, keepdims=True)
    return (values - mean) * lax.rsqrt(var + 1e-05) * gain + bias


def body(pair, pair_mask, ln_gain, ln_bias, w_proj, w_gate, tri_gain, tri_bias, w_out):
    hidden = w_out.shape[0]
    normed = layer_norm(pair.astype(jnp.float32), ln_gain, ln_bias, -1).astype(jnp.bfloat16)
    proj = jnp.einsum("rkc,cd->drk", normed, w_proj, preferred_element_type=jnp.float32)
    maskf = pair_mask.astype(jnp.float32)
    left = (jax.nn.sigmoid(proj[0:hidden]) * proj[hidden : 2 * hidden] * maskf).astype(jnp.bfloat16)
    right = (
        jax.nn.sigmoid(proj[2 * hidden : 3 * hidden]) * proj[3 * hidden : 4 * hidden] * maskf
    ).astype(jnp.bfloat16)
    left_all, right_all = (
        lax.all_to_all(left, "dap", split_axis=0, concat_axis=1, tiled=True),
        lax.all_to_all(right, "dap", split_axis=0, concat_axis=1, tiled=True),
    )
    out_gate = jax.nn.sigmoid(
        jnp.einsum("rjc,cd->rjd", normed, w_gate, preferred_element_type=jnp.float32)
    )
    partial_value = jnp.einsum(
        "hjk,hik->hij", right_all, left_all, preferred_element_type=jnp.float32
    ).astype(jnp.bfloat16)
    moved = lax.all_to_all(partial_value, "dap", split_axis=1, concat_axis=0, tiled=True)
    tri = lax.psum_scatter(
        moved.astype(jnp.float32).astype(jnp.bfloat16), "sub", scatter_dimension=2, tiled=True
    )
    tri_normed = layer_norm(
        tri.astype(jnp.float32), tri_gain[:, None, None], tri_bias[:, None, None], 0
    ).astype(jnp.bfloat16)
    linear = jnp.einsum("crj,cd->rjd", tri_normed, w_out, preferred_element_type=jnp.float32)
    return (out_gate * linear).astype(jnp.bfloat16)


def sigmoid(x):
    return 0.5 * jnp.tanh(0.5 * x) + 0.5


def nt_dot(a, b):
    return lax.dot_general(a, b, (((1,), (1,)), ((), ())), preferred_element_type=jnp.float32)


def kernel(
    n, pair_hbm, mask_hbm, vec_refs, w_proj_hbm, w_gate_hbm, w_out_hbm, out_v,
    pair_v, mask_v, vec_v, w_proj_v, w_gate_v, w_out_v,
    send_e, recv_o, recv_x, send_t, recv_t, stage, gate_v, col_v,
    in_sems, o_sems, x_sems, t_sems,
):
    me = lax.axis_index("dap")
    rows, k, hidden = pair_v.shape[0], pair_v.shape[1], w_out_v.shape[0]
    half = n // 2
    base, place = me // half * half, lax.rem(me, half)

    def load(src, dst, i):
        copy = pltpu.make_async_copy(src, dst, in_sems.at[i])
        copy.start()
        return copy

    def each_other(act):
        @pl.loop(0, half)
        def _(s):
            to = lax.rem(place + s, half)
            act(half - base + to, to)

    def each_own(act):
        @pl.loop(1, half)
        def _(s):
            to = lax.rem(place + s, half)
            act(base + to, to)

    def greet(to, _):
        pl.semaphore_signal(barrier, inc=1, device_id={"dap": to}, device_id_type=MESH)

    barrier = pltpu.get_barrier_semaphore()
    pair_in = load(pair_hbm, pair_v, 0)
    proj_in = load(w_proj_hbm, w_proj_v, 1)
    each_other(greet)
    each_own(greet)
    vec_in = [load(r, vec_v.at[pl.ds(i, 1)], 5 + i) for i, r in enumerate(vec_refs)]
    mask_in = load(mask_hbm, mask_v, 2)
    gate_in = load(w_gate_hbm, w_gate_v, 3)
    out_in = load(w_out_hbm, w_out_v, 4)

    def sender(send, recv, sems):
        def act(to, to_place):
            pltpu.make_async_remote_copy(
                src_ref=send.at[to_place],
                dst_ref=recv.at[place],
                send_sem=sems.at[0],
                recv_sem=sems.at[1],
                device_id={"dap": to},
                device_id_type=MESH,
            ).start()

        return act

    def wait_blocks(recv, sem, count):
        span = recv.at[pl.ds(0, count)]
        pltpu.make_async_copy(span, span, sem).wait()

    proj_in.wait()
    w_t = w_proj_v[...].T
    pair_in.wait()
    for copy in vec_in:
        copy.wait()
    mask_in.wait()
    gain, bias = vec_v[0:1, :], vec_v[1:2, :]

    def edge(proj, mask):
        return sigmoid(proj[0:hidden]) * proj[hidden : 2 * hidden] * mask

    lefts, rights = [], []
    for r in range(rows):
        x = pair_v[r].astype(jnp.float32)
        centred = x - jnp.mean(x, axis=1, keepdims=True)
        var = jnp.mean(centred * centred, axis=1, keepdims=True)
        normed = (centred * lax.rsqrt(var + 1e-05) * gain + bias).astype(jnp.bfloat16)
        pair_v[r] = normed
        proj = nt_dot(w_t, normed)
        mask = mask_v[r : r + 1, :].astype(jnp.float32)
        lefts.append(edge(proj[0 : 2 * hidden], mask).reshape(half, OWNED, k))
        rights.append(edge(proj[2 * hidden : 4 * hidden], mask).reshape(half, OWNED, k))
    send_e[:, 0] = jnp.concatenate(rights, axis=1).astype(jnp.bfloat16)
    send_e[:, 1] = jnp.concatenate(lefts, axis=1).astype(jnp.bfloat16)
    pl.semaphore_wait(barrier, n - 1)
    each_own(sender(send_e, recv_o, o_sems))
    each_other(sender(send_e.at[:, 0], recv_x, x_sems))
    recv_o[place] = send_e[place]

    gate_in.wait()
    for r in range(rows):
        gate_v[r] = sigmoid(jnp.dot(pair_v[r], w_gate_v[...], preferred_element_type=jnp.float32))
    for i in range(2):
        col_v[i] = jnp.broadcast_to(vec_v[2 + i : 3 + i, :], (k, hidden)).T
    out_in.wait()

    ours = half * rows
    size = ours * OWNED

    def spread(start, blocks):
        stage[pl.ds(pl.multiple_of(start * rows * OWNED, size), size)] = blocks.astype(jnp.float32).reshape(size, k)

    wait_blocks(recv_o, o_sems.at[1], half - 1)
    spread(0, recv_o[:, 1])
    area = stage.at[pl.ds(0, size)]
    lefts = [area[pl.ds(c, ours, stride=OWNED), :].astype(jnp.bfloat16) for c in range(OWNED)]
    spread(base, recv_o[:, 0])
    wait_blocks(recv_x, x_sems.at[1], half)
    spread(half - base, recv_x[...])
    rights = [stage[pl.ds(c, n * rows, stride=OWNED), :].astype(jnp.bfloat16) for c in range(OWNED)]
    few = half // 2
    for part in range(2):
        span = few * rows
        cut = stage.at[pl.ds(part * span * OWNED, span * OWNED)]
        for c in range(OWNED):
            cut[pl.ds(c, span, stride=OWNED), :] = nt_dot(lefts[c][part * span : (part + 1) * span], rights[c])
        send_t[pl.ds(part * few, few)] = cut[...].astype(jnp.bfloat16).reshape(few, rows * OWNED, k)

        @pl.loop(0, few)
        def _(s):
            to = part * few + lax.rem(place + s, few)

            @pl.when(to != place)
            def _():
                sender(send_t, recv_t, t_sems)(base + to, to)

    recv_t[place] = send_t[place]

    wait_blocks(recv_t, t_sems.at[1], half - 1)
    tri = recv_t[...].astype(jnp.float32)
    for r in range(rows):
        t = tri[:, r * OWNED : (r + 1) * OWNED].reshape(hidden, k)
        centred = t - jnp.mean(t, axis=0, keepdims=True)
        var = jnp.mean(centred * centred, axis=0, keepdims=True)
        normed = (centred * lax.rsqrt(var + 1e-05) * col_v[0] + col_v[1]).astype(jnp.bfloat16)
        linear = lax.dot_general(
            normed, w_out_v[...], (((0,), (0,)), ((), ())), preferred_element_type=jnp.float32
        )
        out_v[r] = (gate_v[r] * linear).astype(jnp.bfloat16)
    wait_blocks(recv_o, o_sems.at[0], half - 1)
    wait_blocks(recv_x, x_sems.at[0], half)
    wait_blocks(recv_t, t_sems.at[0], half - 1)


def fused(n, pair, pair_mask, ln_gain, ln_bias, w_proj, w_gate, tri_gain, tri_bias, w_out):
    rows, k, c = pair.shape
    hidden = w_out.shape[0]
    bf16, f32 = jnp.bfloat16, jnp.float32
    vecs = [v.reshape(1, -1) for v in (ln_gain, ln_bias, tri_gain, tri_bias)]
    hbm_spec = pl.BlockSpec(memory_space=pltpu.HBM)

    def run(pair_r, mask_r, g1, b1, g2, b2, wp, wg, wo, out_r, *scratch):
        kernel(n, pair_r, mask_r, (g1, b1, g2, b2), wp, wg, wo, out_r, *scratch)

    return pl.pallas_call(
        run,
        out_shape=jax.ShapeDtypeStruct((rows, k, c), bf16),
        in_specs=[hbm_spec] * 9,
        out_specs=pl.BlockSpec(memory_space=pltpu.VMEM),
        scratch_shapes=[
            pltpu.VMEM((rows, k, c), bf16),
            pltpu.VMEM((rows, k), jnp.int32),
            pltpu.VMEM((8, c), f32),
            pltpu.VMEM(w_proj.shape, bf16),
            pltpu.VMEM(w_gate.shape, bf16),
            pltpu.VMEM(w_out.shape, bf16),
            *[
                pltpu.VMEM((n // 2, *sides, rows * OWNED, k), bf16)
                for sides in ((2,), (2,), (), (), ())
            ],
            pltpu.VMEM((n * rows * OWNED, k), f32),
            pltpu.VMEM((rows, k, c), f32),
            pltpu.VMEM((2, hidden, k), f32),
            pltpu.SemaphoreType.DMA((9,)),
            pltpu.SemaphoreType.DMA((2,)),
            pltpu.SemaphoreType.DMA((2,)),
            pltpu.SemaphoreType.DMA((2,)),
        ],
        compiler_params=pltpu.CompilerParams(
            collective_id=0, has_side_effects=True, vmem_limit_bytes=16 * 2**20
        ),
    )(*[pltpu.with_memory_space_constraint(x, pltpu.HBM) for x in (pair, pair_mask, *vecs, w_proj, w_gate, w_out)])


def fits(mesh, pair, w_out):
    n = mesh.shape["dap"]
    rows, k, c = pair.shape
    hidden = w_out.shape[0]
    return (
        mesh.shape["sub"] == 1
        and n % 4 == 0
        and 2 * hidden == OWNED * n
        and rows * OWNED % 16 == 0
        and k == rows * n
        and k % 128 == 0
        and c == hidden
        and c % 128 == 0
    )


def solution(mesh):
    placed = (
        P(("grp", "dap"), "sub", None),
        P(("grp", "dap"), "sub"),
        P(),
        P(),
        P(),
        P(),
        P(),
        P(),
        P(),
    )

    def local(pair, *rest):
        if fits(mesh, pair, rest[-1]):
            return fused(mesh.shape["dap"], pair, *rest)
        return body(pair, *rest)

    return jax.shard_map(
        local, mesh=mesh, in_specs=placed, out_specs=P(("grp", "dap"), "sub", None), check_vma=False
    )
```
